32 devices in a mesh: groups: 2 (over y), video: 8 (over z, x), fsdp: 2 (over core).
Axes of the slice: x: 2, y: 2, z: 4, core: 2. Of those that a mesh axis runs over, the one named last changes fastest.
Arguments:
- video: bfloat16 [32, 32, 16, 512], P(('groups', 'video', 'fsdp')), parts along dimension 0, may hold values from -6 to 6
- w_spatial: bfloat16 [3, 3, 512, 512], P(None, None, 'fsdp'), may hold values from -0.09375 to 0.09375
- norm_gain: float32 [512], replicated, may hold values from 0.1 to 1.9
- norm_shift: float32 [512], replicated, may hold values from -3 to 3
- w_time: bfloat16 [3, 512, 512], P(None, 'fsdp'), may hold values from -0.15625 to 0.15625
Outputs:
- result: bfloat16 [32, 32, 16, 512], P(('groups', 'video', 'fsdp')), parts along dimension 0
The draws below stay inside these ranges and needn't reach their ends.
There are 2 independent parts, one for each index of `groups`. The reference program is written for one: setup_inputs(seed, part) draws one part's arguments, and reference() takes and returns one part's arrays. A program takes and returns all parts, laid end to end along the dimension named above; an argument that names none is the same for every part. Nothing has to cross between parts.
All inputs are finite; a program needn't handle non-finite values.
Results may differ from the reference program's by a relative error of at most 0.0049.
Values may be sent and summed in bfloat16 or wider, within the bound.
A program may use at most 64 MiB of HBM per device.

```python
import jax
import jax.numpy as jnp
from jax import lax

CHANNELS = 512
GROUPS = 32
CLIP = 16
HEIGHT = 32
WIDTH = 16
FRAMES = 16


def level_of(own_key, dims, split, low, top_value):
    def one(dim, shards_of):
        heights = jax.random.uniform(jax.random.fold_in(jax.random.fold_in(own_key, 6), dim), (shards_of,), jnp.float32, low / len(split), top_value / len(split))
        return jnp.repeat(jnp.exp(heights), dims[dim] // shards_of).reshape((-1,) + (1,) * (len(dims) - dim - 1))

    factor_of = one(*split[0])
    for cut in split[1:]:
        factor_of = factor_of * one(*cut)
    return factor_of


def noise(own_key, dims, deviation, most, split=(), dtype=jnp.bfloat16):
    drawn = deviation * jax.random.normal(own_key, dims, jnp.float32)
    if split:
        drawn = drawn * level_of(own_key, dims, split, -0.22, 0.18)
    return jnp.clip(drawn, -most, most).astype(dtype)


def setup_inputs(seed: int = 0, part: int = 0) -> dict:
    seeds = jax.random.split(jax.random.key(seed), 6)
    part_keys = jax.random.split(jax.random.fold_in(seeds[5], part), 6)
    video = noise(part_keys[0], (FRAMES, HEIGHT, WIDTH, CHANNELS), 1.0, 6.0, ((0, 16),))
    w_spatial = noise(seeds[1], (3, 3, CHANNELS, CHANNELS), (9 * CHANNELS) ** -0.5, 0.09375, ((2, 2),))
    norm_gain = jnp.clip(1.0 + 0.18 * jax.random.normal(seeds[2], (CHANNELS,), jnp.float32), 0.1, 1.9)
    norm_shift = noise(seeds[3], (CHANNELS,), 0.5, 3.0, (), jnp.float32)
    w_time = noise(seeds[4], (3, CHANNELS, CHANNELS), (3 * CHANNELS) ** -0.5, 0.15625, ((1, 2),))
    return {"video": video, "w_spatial": w_spatial, "norm_gain": norm_gain, "norm_shift": norm_shift, "w_time": w_time}


def reference(video, w_spatial, norm_gain, norm_shift, w_time):
    count, height, width, channels = video.shape
    spatial = lax.conv_general_dilated(video, w_spatial, (1, 1), ((1, 1), (1, 1)), dimension_numbers=('NHWC', 'HWIO', 'NHWC'), preferred_element_type=jnp.float32)
    grouped = spatial.reshape(count, height * width, GROUPS, channels // GROUPS)
    mean = lax.optimization_barrier(jnp.mean(grouped, axis=(1, 3), keepdims=True))
    variance = lax.optimization_barrier(jnp.mean(jnp.square(grouped - mean), axis=(1, 3), keepdims=True))
    normed = ((grouped - mean) * lax.rsqrt(variance + 1e-05)).reshape(count, height * width, channels)
    hidden = jax.nn.silu(normed * norm_gain + norm_shift).astype(jnp.bfloat16)
    clips = hidden.reshape(count // CLIP, CLIP, height * width, channels)
    padded = jnp.pad(clips, ((0, 0), (1, 1), (0, 0), (0, 0)))
    total = jnp.zeros((count * height * width, channels), jnp.float32)
    for tap in range(3):
        shifted = padded[:, tap:tap + CLIP].reshape(-1, channels)
        total = total + jnp.dot(shifted, w_time[tap], preferred_element_type=jnp.float32)
    result = hidden.reshape(-1, channels).astype(jnp.float32) + total
    return result.astype(jnp.bfloat16).reshape(count, height, width, channels)
```

```python
import functools

import jax
import jax.numpy as jnp
from jax import lax
from jax.experimental import pallas as pl
from jax.experimental.pallas import tpu as pltpu
from jax.sharding import PartitionSpec as P

GROUPS = 32
CLIP = 16
MESH = pl.DeviceIdType.MESH
CHUNK = 256


def kernel(
    width,
    group_size,
    video_ref,
    ws_ref,
    gain_ref,
    shift_ref,
    wt_ref,
    out_ref,
    raw,
    xs,
    ws,
    wt,
    acc,
    hid,
    near,
    far,
    local_sem,
    w_send,
    w_recv,
    near_send,
    near_recv,
    far_send,
    far_recv,
):
    rows = raw.shape[0]
    half = wt.shape[2]
    blocks = 2
    group = lax.axis_index("groups")
    block = lax.axis_index("video")
    side = lax.axis_index("fsdp")
    other = 1 - side
    position = (block * 2 + side) % CLIP
    has_far = position != side * (CLIP - 1)
    partner = (group, block, other)
    far_block = jnp.where(has_far, block + 2 * side - 1, block)
    distant = (group, far_block, other)

    video_copy = pltpu.make_async_copy(video_ref, raw, local_sem.at[0])
    ws_copy = pltpu.make_async_copy(ws_ref, ws.at[side], local_sem.at[1])
    wt_copy = pltpu.make_async_copy(wt_ref, wt.at[side], local_sem.at[2])
    video_copy.start()
    ws_copy.start()
    wt_copy.start()

    barrier = pltpu.get_barrier_semaphore()
    pl.semaphore_signal(barrier, inc=1, device_id=partner, device_id_type=MESH)

    @pl.when(has_far)
    def _():
        pl.semaphore_signal(barrier, inc=1, device_id=distant, device_id_type=MESH)

    pl.semaphore_wait(barrier, 1 + has_far.astype(jnp.int32))

    w_copies = []
    for nb in range(blocks):
        columns = pl.ds(nb * half, half)
        w_copies.append(
            pltpu.make_async_remote_copy(
                src_ref=ws_ref.at[:, :, columns],
                dst_ref=ws.at[side, :, :, columns],
                send_sem=w_send.at[nb],
                recv_sem=w_recv.at[nb],
                device_id=partner,
                device_id_type=MESH,
            )
        )
    w_copies.append(
        pltpu.make_async_remote_copy(
            src_ref=wt_ref,
            dst_ref=wt.at[side],
            send_sem=w_send.at[blocks],
            recv_sem=w_recv.at[blocks],
            device_id=partner,
            device_id_type=MESH,
        )
    )
    for copy in w_copies:
        copy.start()

    video_copy.wait()
    column = lax.broadcasted_iota(jnp.int32, (rows, half), 0) % width
    for h in range(blocks):
        centre = raw[:, h * half : (h + 1) * half]
        wide = centre.astype(jnp.float32)
        before = jnp.where(column != 0, pltpu.roll(wide, 1, 0), 0.0)
        after = jnp.where(column != width - 1, pltpu.roll(wide, rows - 1, 0), 0.0)
        edge = jnp.zeros((width, 3 * half), jnp.bfloat16)
        xs[h, 0:width, :] = edge
        xs[h, width + rows : 2 * width + rows, :] = edge
        xs[h, width : width + rows, 0:half] = before.astype(jnp.bfloat16)
        xs[h, width : width + rows, half : 2 * half] = centre
        xs[h, width : width + rows, 2 * half : 3 * half] = after.astype(jnp.bfloat16)

    def conv(h, nb, first):
        def step(m, carry):
            start = pl.multiple_of(m * CHUNK, CHUNK)
            total = None
            for dy in range(3):
                part = jnp.dot(
                    xs[h, pl.ds(start + dy * width, CHUNK), :],
                    ws[h, dy, :, nb * half : (nb + 1) * half],
                    preferred_element_type=jnp.float32,
                )
                total = part if total is None else total + part
            if not first:
                total = total + acc[nb, pl.ds(start, CHUNK), :]
            acc[nb, pl.ds(start, CHUNK), :] = total
            return carry

        lax.fori_loop(0, rows // CHUNK, step, 0)

    ws_copy.wait()
    for nb in range(blocks):
        conv(side, nb, True)

    same = (
        lax.broadcasted_iota(jnp.int32, (half, half), 0) // group_size
        == lax.broadcasted_iota(jnp.int32, (half, half), 1) // group_size
    ).astype(jnp.float32)

    def spread(sums):
        wide = jnp.broadcast_to(sums, (8, half))
        total = jnp.dot(
            wide, same, preferred_element_type=jnp.float32, precision=lax.Precision.HIGHEST
        )
        return total[0:1] / (rows * group_size)

    h_copies = []
    for nb in range(blocks):
        w_copies[nb].wait_recv()
        conv(other, nb, False)
        mean = spread(jnp.sum(acc[nb], axis=0, keepdims=True))
        variance = spread(jnp.sum(jnp.square(acc[nb] - mean), axis=0, keepdims=True))
        span = slice(nb * half, (nb + 1) * half)
        scale = lax.rsqrt(variance + 1e-05) * gain_ref[:, span]
        v = (acc[nb] - mean) * scale + shift_ref[:, span]
        hid[nb] = (v / (1.0 + jnp.exp(-v))).astype(jnp.bfloat16)
        near_copy = pltpu.make_async_remote_copy(
            src_ref=hid.at[nb],
            dst_ref=near.at[nb],
            send_sem=near_send.at[nb],
            recv_sem=near_recv.at[nb],
            device_id=partner,
            device_id_type=MESH,
        )
        far_copy = pltpu.make_async_remote_copy(
            src_ref=hid.at[nb],
            dst_ref=far.at[nb],
            send_sem=far_send.at[nb],
            recv_sem=far_recv.at[nb],
            device_id=distant,
            device_id_type=MESH,
        )

        @pl.when(has_far)
        def _():
            far_copy.start()

        near_copy.start()
        h_copies.append((near_copy, far_copy))

    def mix(frame, tap, nb):
        def step(m, carry):
            spot = pl.ds(pl.multiple_of(m * CHUNK, CHUNK), CHUNK)
            for ob in range(blocks):
                part = jnp.dot(
                    frame[nb, spot, :],
                    wt[nb, tap, :, ob * half : (ob + 1) * half],
                    preferred_element_type=jnp.float32,
                )
                acc[ob, spot, :] = acc[ob, spot, :] + part
            return carry

        lax.fori_loop(0, rows // CHUNK, step, 0)

    wt_copy.wait()
    w_copies[blocks].wait_recv()
    for nb in range(blocks):
        acc[nb] = hid[nb].astype(jnp.float32)
    for nb in range(blocks):
        mix(hid, 1, nb)
    for nb in range(blocks):
        h_copies[nb][0].wait_recv()
        mix(near, 2 * other, nb)

    @pl.when(has_far)
    def _():
        for nb in range(blocks):
            h_copies[nb][1].wait_recv()
            mix(far, 2 * side, nb)

    for nb in range(blocks):
        out_ref[:, nb * half : (nb + 1) * half] = acc[nb].astype(jnp.bfloat16)

    for copy in w_copies:
        copy.wait_send()
    for nb in range(blocks):
        h_copies[nb][0].wait_send()

    @pl.when(has_far)
    def _():
        for nb in range(blocks):
            h_copies[nb][1].wait_send()


def body(video, w_spatial, norm_gain, norm_shift, w_time):
    count, height, width, channels = video.shape
    half = w_time.shape[1]
    assert count == 1 and 2 * half == channels
    rows = height * width
    bf16 = jnp.bfloat16
    vmem = pl.BlockSpec(memory_space=pltpu.VMEM)
    hbm = pl.BlockSpec(memory_space=pl.ANY)
    dma = pltpu.SemaphoreType.DMA
    out = pl.pallas_call(
        functools.partial(kernel, width, channels // GROUPS),
        out_shape=jax.ShapeDtypeStruct((rows, channels), bf16),
        in_specs=[hbm, hbm, vmem, vmem, hbm],
        out_specs=vmem,
        scratch_shapes=[
            pltpu.VMEM((rows, channels), bf16),
            pltpu.VMEM((2, rows + 2 * width, 3 * half), bf16),
            pltpu.VMEM((2, 3, 3 * half, channels), bf16),
            pltpu.VMEM((2, 3, half, channels), bf16),
            pltpu.VMEM((2, rows, half), jnp.float32),
            pltpu.VMEM((2, rows, half), bf16),
            pltpu.VMEM((2, rows, half), bf16),
            pltpu.VMEM((2, rows, half), bf16),
            dma((3,)),
            dma((3,)),
            dma((3,)),
            dma((2,)),
            dma((2,)),
            dma((2,)),
            dma((2,)),
        ],
        compiler_params=pltpu.CompilerParams(
            collective_id=0, has_side_effects=True, vmem_limit_bytes=48 * 1024 * 1024
        ),
    )(
        video.reshape(rows, channels),
        w_spatial.reshape(3, 3 * half, channels),
        norm_gain.reshape(1, channels),
        norm_shift.reshape(1, channels),
        w_time,
    )
    return out.reshape(video.shape)


def solution(mesh):
    placed = (
        P(("groups", "video", "fsdp"), None, None, None),
        P(None, None, "fsdp", None),
        P(),
        P(),
        P(None, "fsdp", None),
    )
    return jax.shard_map(
        body,
        mesh=mesh,
        in_specs=placed,
        out_specs=P(("groups", "video", "fsdp"), None, None, None),
        check_vma=False,
    )
```

```python
import functools

import jax
import jax.numpy as jnp
from jax import lax
from jax.experimental import pallas as pl
from jax.experimental.pallas import tpu as pltpu
from jax.sharding import PartitionSpec as P

GROUPS = 32
CLIP = 16
MESH = pl.DeviceIdType.MESH
CHUNK = 256
PARTS = 4


def kernel(
    width,
    group_size,
    video_ref,
    ws_ref,
    gain_hbm,
    shift_hbm,
    wt_ref,
    out_ref,
    raw,
    xs,
    ws,
    wt,
    acc,
    hid,
    near,
    gain_ref,
    shift_ref,
    far_raw,
    far_xs,
    stats,
    far_stats,
    local_sem,
    w_send,
    w_recv,
    near_send,
    near_recv,
    far_send,
    far_recv,
    stat_send,
    stat_recv,
):
    rows = raw.shape[0]
    half = wt.shape[2]
    blocks = 2
    group = lax.axis_index("groups")
    block = lax.axis_index("video")
    side = lax.axis_index("fsdp")
    other = 1 - side
    position = (block * 2 + side) % CLIP
    has_far = position != side * (CLIP - 1)
    partner = (group, block, other)
    far_block = jnp.where(has_far, block + 2 * side - 1, block)
    distant = (group, far_block, other)

    video_copy = pltpu.make_async_copy(video_ref, raw, local_sem.at[0])
    ws_copy = pltpu.make_async_copy(ws_ref, ws.at[side], local_sem.at[1])
    wt_copy = pltpu.make_async_copy(wt_ref, wt.at[side], local_sem.at[2])
    gain_copy = pltpu.make_async_copy(gain_hbm, gain_ref, local_sem.at[3])
    shift_copy = pltpu.make_async_copy(shift_hbm, shift_ref, local_sem.at[4])
    video_copy.start()
    ws_copy.start()
    wt_copy.start()
    gain_copy.start()
    shift_copy.start()

    barrier = pltpu.get_barrier_semaphore()
    pl.semaphore_signal(barrier, inc=1, device_id=partner, device_id_type=MESH)

    @pl.when(has_far)
    def _():
        pl.semaphore_signal(barrier, inc=1, device_id=distant, device_id_type=MESH)

    pl.semaphore_wait(barrier, 1 + has_far.astype(jnp.int32))

    step_rows = rows // PARTS
    bounds = [0] + [step_rows * p + width for p in range(1, PARTS)] + [rows]
    far_copies = []
    for p in range(PARTS):
        span = pl.ds(bounds[p], bounds[p + 1] - bounds[p])
        far_copies.append(
            pltpu.make_async_remote_copy(
                src_ref=video_ref.at[span],
                dst_ref=far_raw.at[span],
                send_sem=far_send.at[p],
                recv_sem=far_recv.at[p],
                device_id=distant,
                device_id_type=MESH,
            )
        )

    @pl.when(has_far)
    def _():
        for copy in far_copies:
            copy.start()

    w_copies = []
    for nb in range(blocks):
        columns = pl.ds(nb * half, half)
        w_copies.append(
            pltpu.make_async_remote_copy(
                src_ref=ws_ref.at[:, :, columns],
                dst_ref=ws.at[side, :, :, columns],
                send_sem=w_send.at[nb],
                recv_sem=w_recv.at[nb],
                device_id=partner,
                device_id_type=MESH,
            )
        )
    w_copies.append(
        pltpu.make_async_remote_copy(
            src_ref=wt_ref,
            dst_ref=wt.at[side],
            send_sem=w_send.at[blocks],
            recv_sem=w_recv.at[blocks],
            device_id=partner,
            device_id_type=MESH,
        )
    )
    for copy in w_copies:
        copy.start()

    video_copy.wait()

    def taps(source, target, low, high):
        count = high - low
        column = lax.broadcasted_iota(jnp.int32, (count, half), 0) % width
        for h in range(blocks):
            centre = source[low:high, h * half : (h + 1) * half]
            wide = centre.astype(jnp.float32)
            before = jnp.where(column != 0, pltpu.roll(wide, 1, 0), 0.0)
            after = jnp.where(column != width - 1, pltpu.roll(wide, count - 1, 0), 0.0)
            here = slice(width + low, width + high)
            target[h, here, 0:half] = before.astype(jnp.bfloat16)
            target[h, here, half : 2 * half] = centre
            target[h, here, 2 * half : 3 * half] = after.astype(jnp.bfloat16)

    def edges(target):
        edge = jnp.zeros((width, 3 * half), jnp.bfloat16)
        for h in range(blocks):
            target[h, 0:width, :] = edge
            target[h, width + rows : 2 * width + rows, :] = edge

    edges(xs)
    edges(far_xs)
    taps(raw, xs, 0, rows)

    def conv(h, nb, first):
        def step(m, carry):
            start = pl.multiple_of(m * CHUNK, CHUNK)
            total = None
            for dy in range(3):
                part = jnp.dot(
                    xs[h, pl.ds(start + dy * width, CHUNK), :],
                    ws[h, dy, :, nb * half : (nb + 1) * half],
                    preferred_element_type=jnp.float32,
                )
                total = part if total is None else total + part
            if not first:
                total = total + acc[nb, pl.ds(start, CHUNK), :]
            acc[nb, pl.ds(start, CHUNK), :] = total
            return carry

        lax.fori_loop(0, rows // CHUNK, step, 0)

    ws_copy.wait()
    for nb in range(blocks):
        conv(side, nb, True)

    same = (
        lax.broadcasted_iota(jnp.int32, (half, half), 0) // group_size
        == lax.broadcasted_iota(jnp.int32, (half, half), 1) // group_size
    ).astype(jnp.float32)

    def spread(sums):
        wide = jnp.broadcast_to(sums, (8, half))
        total = jnp.dot(
            wide, same, preferred_element_type=jnp.float32, precision=lax.Precision.HIGHEST
        )
        return total[0:1] / (rows * group_size)

    stat_copy = pltpu.make_async_remote_copy(
        src_ref=stats,
        dst_ref=far_stats,
        send_sem=stat_send.at[0],
        recv_sem=stat_recv.at[0],
        device_id=distant,
        device_id_type=MESH,
    )
    gain_copy.wait()
    shift_copy.wait()
    h_copies = []
    for nb in range(blocks):
        w_copies[nb].wait_recv()
        conv(other, nb, False)
        mean = spread(jnp.sum(acc[nb], axis=0, keepdims=True))
        variance = spread(jnp.sum(jnp.square(acc[nb] - mean), axis=0, keepdims=True))
        span = slice(nb * half, (nb + 1) * half)
        scale = lax.rsqrt(variance + 1e-05) * gain_ref[:, span]
        v = (acc[nb] - mean) * scale + shift_ref[:, span]
        hid[nb] = (v / (1.0 + jnp.exp(-v))).astype(jnp.bfloat16)
        near_copy = pltpu.make_async_remote_copy(
            src_ref=hid.at[nb],
            dst_ref=near.at[nb],
            send_sem=near_send.at[nb],
            recv_sem=near_recv.at[nb],
            device_id=partner,
            device_id_type=MESH,
        )
        near_copy.start()
        h_copies.append(near_copy)
        stats[nb, 0] = jnp.broadcast_to(mean, (8, half))
        stats[nb, 1] = jnp.broadcast_to(scale, (8, half))

    @pl.when(has_far)
    def _():
        stat_copy.start()

    def mix(frame, tap, nb):
        def step(m, carry):
            spot = pl.ds(pl.multiple_of(m * CHUNK, CHUNK), CHUNK)
            for ob in range(blocks):
                part = jnp.dot(
                    frame[nb, spot, :],
                    wt[nb, tap, :, ob * half : (ob + 1) * half],
                    preferred_element_type=jnp.float32,
                )
                acc[ob, spot, :] = acc[ob, spot, :] + part
            return carry

        lax.fori_loop(0, rows // CHUNK, step, 0)

    wt_copy.wait()
    w_copies[blocks].wait_recv()
    for nb in range(blocks):
        acc[nb] = hid[nb].astype(jnp.float32)
    for nb in range(blocks):
        mix(hid, 1, nb)

    def far_part(p):
        far_copies[p].wait_recv()
        taps(far_raw, far_xs, bounds[p], bounds[p + 1])
        low = p * step_rows
        here = slice(low, low + step_rows)
        if p == 0:
            stat_copy.wait_recv()
        for nb in range(blocks):
            total = None
            for h in range(blocks):
                for dy in range(3):
                    part = jnp.dot(
                        far_xs[h, low + dy * width : low + dy * width + step_rows, :],
                        ws[h, dy, :, nb * half : (nb + 1) * half],
                        preferred_element_type=jnp.float32,
                    )
                    total = part if total is None else total + part
            v = (total - far_stats[nb, 0, 0:1]) * far_stats[nb, 1, 0:1]
            v = v + shift_ref[:, nb * half : (nb + 1) * half]
            frame = (v / (1.0 + jnp.exp(-v))).astype(jnp.bfloat16)
            for ob in range(blocks):
                acc[ob, here, :] = acc[ob, here, :] + jnp.dot(
                    frame,
                    wt[nb, 2 * side, :, ob * half : (ob + 1) * half],
                    preferred_element_type=jnp.float32,
                )

    for nb in range(blocks):
        h_copies[nb].wait_recv()
        mix(near, 2 * other, nb)

    @pl.when(has_far)
    def _():
        for p in range(PARTS):
            far_part(p)

    for nb in range(blocks):
        out_ref[:, nb * half : (nb + 1) * half] = acc[nb].astype(jnp.bfloat16)

    for copy in w_copies + h_copies:
        copy.wait_send()

    @pl.when(has_far)
    def _():
        for copy in far_copies:
            copy.wait_send()
        stat_copy.wait_send()


def body(video, w_spatial, norm_gain, norm_shift, w_time):
    count, height, width, channels = video.shape
    half = w_time.shape[1]
    assert count == 1 and 2 * half == channels
    rows = height * width
    bf16 = jnp.bfloat16
    vmem = pl.BlockSpec(memory_space=pltpu.VMEM)
    hbm = pl.BlockSpec(memory_space=pltpu.HBM)
    dma = pltpu.SemaphoreType.DMA
    out = pl.pallas_call(
        functools.partial(kernel, width, channels // GROUPS),
        out_shape=jax.ShapeDtypeStruct((rows, channels), bf16),
        in_specs=[hbm] * 5,
        out_specs=vmem,
        scratch_shapes=[
            pltpu.VMEM((rows, channels), bf16),
            pltpu.VMEM((2, rows + 2 * width, 3 * half), bf16),
            pltpu.VMEM((2, 3, 3 * half, channels), bf16),
            pltpu.VMEM((2, 3, half, channels), bf16),
            pltpu.VMEM((2, rows, half), jnp.float32),
            pltpu.VMEM((2, rows, half), bf16),
            pltpu.VMEM((2, rows, half), bf16),
            pltpu.VMEM((1, channels), jnp.float32),
            pltpu.VMEM((1, channels), jnp.float32),
            pltpu.VMEM((rows, channels), bf16),
            pltpu.VMEM((2, rows + 2 * width, 3 * half), bf16),
            pltpu.VMEM((2, 2, 8, half), jnp.float32),
            pltpu.VMEM((2, 2, 8, half), jnp.float32),
            dma((5,)),
            dma((3,)),
            dma((3,)),
            dma((2,)),
            dma((2,)),
            dma((PARTS,)),
            dma((PARTS,)),
            dma((1,)),
            dma((1,)),
        ],
        compiler_params=pltpu.CompilerParams(
            collective_id=0, has_side_effects=True, vmem_limit_bytes=63 * 1024 * 1024
        ),
    )(
        video.reshape(rows, channels),
        w_spatial.reshape(3, 3 * half, channels),
        norm_gain.reshape(1, channels),
        norm_shift.reshape(1, channels),
        w_time,
    )
    return out.reshape(video.shape)


def solution(mesh):
    placed = (
        P(("groups", "video", "fsdp"), None, None, None),
        P(None, None, "fsdp", None),
        P(),
        P(),
        P(None, "fsdp", None),
    )
    return jax.shard_map(
        body,
        mesh=mesh,
        in_specs=placed,
        out_specs=P(("groups", "video", "fsdp"), None, None, None),
        check_vma=False,
    )
```

```python
import functools

import jax
import jax.numpy as jnp
from jax import lax
from jax.experimental import pallas as pl
from jax.experimental.pallas import tpu as pltpu
from jax.sharding import PartitionSpec as P

GROUPS = 32
CLIP = 16
MESH = pl.DeviceIdType.MESH
CHUNK = 256
PARTS = 1


def kernel(
    width,
    group_size,
    video_ref,
    ws_ref,
    gain_hbm,
    shift_hbm,
    wt_ref,
    out_ref,
    raw,
    xs,
    ws,
    wt,
    acc,
    hid,
    near,
    gain_ref,
    shift_ref,
    far_raw,
    far_xs,
    stats,
    far_stats,
    far_hid,
    local_sem,
    w_send,
    w_recv,
    near_send,
    near_recv,
    far_send,
    far_recv,
    stat_send,
    stat_recv,
    late_send,
    late_recv,
):
    rows = raw.shape[0]
    half = wt.shape[2]
    blocks = 2
    group = lax.axis_index("groups")
    block = lax.axis_index("video")
    side = lax.axis_index("fsdp")
    other = 1 - side
    position = (block * 2 + side) % CLIP
    has_far = position != side * (CLIP - 1)
    partner = (group, block, other)
    far_block = jnp.where(has_far, block + 2 * side - 1, block)
    distant = (group, far_block, other)

    video_copy = pltpu.make_async_copy(video_ref, raw, local_sem.at[0])
    ws_copy = pltpu.make_async_copy(ws_ref, ws.at[side], local_sem.at[1])
    wt_copy = pltpu.make_async_copy(wt_ref, wt.at[side], local_sem.at[2])
    gain_copy = pltpu.make_async_copy(gain_hbm, gain_ref, local_sem.at[3])
    shift_copy = pltpu.make_async_copy(shift_hbm, shift_ref, local_sem.at[4])
    video_copy.start()
    ws_copy.start()
    wt_copy.start()
    gain_copy.start()
    shift_copy.start()

    barrier = pltpu.get_barrier_semaphore()
    pl.semaphore_signal(barrier, inc=1, device_id=partner, device_id_type=MESH)

    @pl.when(has_far)
    def _():
        pl.semaphore_signal(barrier, inc=1, device_id=distant, device_id_type=MESH)

    pl.semaphore_wait(barrier, 1 + has_far.astype(jnp.int32))

    early = rows // 2
    step_rows = early // PARTS
    bounds = [0] + [step_rows * (p + 1) + width for p in range(PARTS)]
    far_copies = []
    for p in range(PARTS):
        span = pl.ds(bounds[p], bounds[p + 1] - bounds[p])
        far_copies.append(
            pltpu.make_async_remote_copy(
                src_ref=video_ref.at[span],
                dst_ref=far_raw.at[span],
                send_sem=far_send.at[p],
                recv_sem=far_recv.at[p],
                device_id=distant,
                device_id_type=MESH,
            )
        )

    @pl.when(has_far)
    def _():
        for copy in far_copies:
            copy.start()

    w_copies = []
    for nb in range(blocks):
        columns = pl.ds(nb * half, half)
        w_copies.append(
            pltpu.make_async_remote_copy(
                src_ref=ws_ref.at[:, columns],
                dst_ref=ws.at[side, :, columns],
                send_sem=w_send.at[nb],
                recv_sem=w_recv.at[nb],
                device_id=partner,
                device_id_type=MESH,
            )
        )
    w_copies.append(
        pltpu.make_async_remote_copy(
            src_ref=wt_ref,
            dst_ref=wt.at[side],
            send_sem=w_send.at[blocks],
            recv_sem=w_recv.at[blocks],
            device_id=partner,
            device_id_type=MESH,
        )
    )
    for copy in w_copies:
        copy.start()

    video_copy.wait()

    def taps(source, target, low, high):
        count = high - low
        column = lax.broadcasted_iota(jnp.int32, (count, half), 0) % width
        for h in range(blocks):
            centre = source[low:high, h * half : (h + 1) * half]
            wide = centre.astype(jnp.float32)
            before = jnp.where(column != 0, pltpu.roll(wide, 1, 0), 0.0)
            after = jnp.where(column != width - 1, pltpu.roll(wide, count - 1, 0), 0.0)
            here = slice(width + low, width + high)
            target[h, here, 0:half] = before.astype(jnp.bfloat16)
            target[h, here, half : 2 * half] = centre
            target[h, here, 2 * half : 3 * half] = after.astype(jnp.bfloat16)

    def edges(target):
        edge = jnp.zeros((width, 3 * half), jnp.bfloat16)
        for h in range(blocks):
            target[h, 0:width, :] = edge
            target[h, width + rows : 2 * width + rows, :] = edge

    edges(xs)
    for h in range(blocks):
        far_xs[h, 0:width, :] = jnp.zeros((width, 3 * half), jnp.bfloat16)
    taps(raw, xs, 0, rows)

    def windows(source, h, start, count):
        return jnp.concatenate(
            [source[h, pl.ds(start + dy * width, count), :] for dy in range(3)], axis=1
        )

    def conv(h, nb, first):
        def step(m, carry):
            start = pl.multiple_of(m * CHUNK, CHUNK)
            total = jnp.dot(
                windows(xs, h, start, CHUNK),
                ws[h, :, nb * half : (nb + 1) * half],
                preferred_element_type=jnp.float32,
            )
            if not first:
                total = total + acc[nb, pl.ds(start, CHUNK), :]
            acc[nb, pl.ds(start, CHUNK), :] = total
            return carry

        lax.fori_loop(0, rows // CHUNK, step, 0)

    ws_copy.wait()
    for nb in range(blocks):
        conv(side, nb, True)

    same = (
        lax.broadcasted_iota(jnp.int32, (half, half), 0) // group_size
        == lax.broadcasted_iota(jnp.int32, (half, half), 1) // group_size
    ).astype(jnp.float32)

    def spread(sums):
        wide = jnp.broadcast_to(sums, (8, half))
        total = jnp.dot(
            wide, same, preferred_element_type=jnp.float32, precision=lax.Precision.HIGHEST
        )
        return total[0:1] / (rows * group_size)

    stat_copies, late_copies = [], []
    for nb in range(blocks):
        stat_copies.append(
            pltpu.make_async_remote_copy(
                src_ref=stats.at[nb],
                dst_ref=far_stats.at[nb],
                send_sem=stat_send.at[nb],
                recv_sem=stat_recv.at[nb],
                device_id=distant,
                device_id_type=MESH,
            )
        )
        late_copies.append(
            pltpu.make_async_remote_copy(
                src_ref=hid.at[nb, pl.ds(early, rows - early)],
                dst_ref=far_hid.at[nb],
                send_sem=late_send.at[nb],
                recv_sem=late_recv.at[nb],
                device_id=distant,
                device_id_type=MESH,
            )
        )
    gain_copy.wait()
    shift_copy.wait()
    h_copies = []
    for nb in range(blocks):
        w_copies[nb].wait_recv()
        conv(other, nb, False)
        mean = spread(jnp.sum(acc[nb], axis=0, keepdims=True))
        variance = spread(jnp.sum(jnp.square(acc[nb] - mean), axis=0, keepdims=True))
        span = slice(nb * half, (nb + 1) * half)
        scale = lax.rsqrt(variance + 1e-05) * gain_ref[:, span]
        stats[nb, 0] = jnp.broadcast_to(mean, (8, half))
        stats[nb, 1] = jnp.broadcast_to(scale, (8, half))

        @pl.when(has_far)
        def _():
            stat_copies[nb].start()

        v = (acc[nb] - mean) * scale + shift_ref[:, span]
        hid[nb] = (v / (1.0 + jnp.exp(-v))).astype(jnp.bfloat16)

        @pl.when(has_far)
        def _():
            late_copies[nb].start()

        near_copy = pltpu.make_async_remote_copy(
            src_ref=hid.at[nb],
            dst_ref=near.at[nb],
            send_sem=near_send.at[nb],
            recv_sem=near_recv.at[nb],
            device_id=partner,
            device_id_type=MESH,
        )
        near_copy.start()
        h_copies.append(near_copy)

    def mix(frame, tap, nb):
        def step(m, carry):
            spot = pl.ds(pl.multiple_of(m * CHUNK, CHUNK), CHUNK)
            for ob in range(blocks):
                part = jnp.dot(
                    frame[nb, spot, :],
                    wt[nb, tap, :, ob * half : (ob + 1) * half],
                    preferred_element_type=jnp.float32,
                )
                acc[ob, spot, :] = acc[ob, spot, :] + part
            return carry

        lax.fori_loop(0, rows // CHUNK, step, 0)

    wt_copy.wait()
    w_copies[blocks].wait_recv()
    for nb in range(blocks):
        acc[nb] = hid[nb].astype(jnp.float32)
    for nb in range(blocks):
        mix(hid, 1, nb)

    def far_part(p):
        far_copies[p].wait_recv()
        taps(far_raw, far_xs, bounds[p], bounds[p + 1])
        low = p * step_rows
        here = slice(low, low + step_rows)
        for nb in range(blocks):
            if p == 0:
                stat_copies[nb].wait_recv()
            total = jnp.dot(
                windows(far_xs, 0, low, step_rows),
                ws[0, :, nb * half : (nb + 1) * half],
                preferred_element_type=jnp.float32,
            ) + jnp.dot(
                windows(far_xs, 1, low, step_rows),
                ws[1, :, nb * half : (nb + 1) * half],
                preferred_element_type=jnp.float32,
            )
            v = (total - far_stats[nb, 0, 0:1]) * far_stats[nb, 1, 0:1]
            v = v + shift_ref[:, nb * half : (nb + 1) * half]
            frame = (v / (1.0 + jnp.exp(-v))).astype(jnp.bfloat16)
            for ob in range(blocks):
                acc[ob, here, :] = acc[ob, here, :] + jnp.dot(
                    frame,
                    wt[nb, 2 * side, :, ob * half : (ob + 1) * half],
                    preferred_element_type=jnp.float32,
                )

    for nb in range(blocks):
        h_copies[nb].wait_recv()
        mix(near, 2 * other, nb)

    @pl.when(has_far)
    def _():
        for p in range(PARTS):
            far_part(p)
        for nb in range(blocks):
            late_copies[nb].wait_recv()
            for ob in range(blocks):
                acc[ob, early:rows, :] = acc[ob, early:rows, :] + jnp.dot(
                    far_hid[nb],
                    wt[nb, 2 * side, :, ob * half : (ob + 1) * half],
                    preferred_element_type=jnp.float32,
                )

    for nb in range(blocks):
        out_ref[:, nb * half : (nb + 1) * half] = acc[nb].astype(jnp.bfloat16)

    for copy in w_copies + h_copies:
        copy.wait_send()

    @pl.when(has_far)
    def _():
        for copy in far_copies + stat_copies + late_copies:
            copy.wait_send()


def body(video, w_spatial, norm_gain, norm_shift, w_time):
    count, height, width, channels = video.shape
    half = w_time.shape[1]
    assert count == 1 and 2 * half == channels
    rows = height * width
    bf16 = jnp.bfloat16
    vmem = pl.BlockSpec(memory_space=pltpu.VMEM)
    hbm = pl.BlockSpec(memory_space=pltpu.HBM)
    dma = pltpu.SemaphoreType.DMA
    out = pl.pallas_call(
        functools.partial(kernel, width, channels // GROUPS),
        out_shape=jax.ShapeDtypeStruct((rows, channels), bf16),
        in_specs=[hbm] * 5,
        out_specs=vmem,
        scratch_shapes=[
            pltpu.VMEM((rows, channels), bf16),
            pltpu.VMEM((2, rows + 2 * width, 3 * half), bf16),
            pltpu.VMEM((2, 9 * half, channels), bf16),
            pltpu.VMEM((2, 3, half, channels), bf16),
            pltpu.VMEM((2, rows, half), jnp.float32),
            pltpu.VMEM((2, rows, half), bf16),
            pltpu.VMEM((2, rows, half), bf16),
            pltpu.VMEM((1, channels), jnp.float32),
            pltpu.VMEM((1, channels), jnp.float32),
            pltpu.VMEM((rows // 2 + width, channels), bf16),
            pltpu.VMEM((2, rows // 2 + 2 * width, 3 * half), bf16),
            pltpu.VMEM((2, 2, 8, half), jnp.float32),
            pltpu.VMEM((2, 2, 8, half), jnp.float32),
            pltpu.VMEM((2, rows - rows // 2, half), bf16),
            dma((5,)),
            dma((3,)),
            dma((3,)),
            dma((2,)),
            dma((2,)),
            dma((PARTS,)),
            dma((PARTS,)),
            dma((2,)),
            dma((2,)),
            dma((2,)),
            dma((2,)),
        ],
        compiler_params=pltpu.CompilerParams(
            collective_id=0, has_side_effects=True, vmem_limit_bytes=63 * 1024 * 1024
        ),
    )(
        video.reshape(rows, channels),
        w_spatial.reshape(9 * half, channels),
        norm_gain.reshape(1, channels),
        norm_shift.reshape(1, channels),
        w_time,
    )
    return out.reshape(video.shape)


def solution(mesh):
    placed = (
        P(("groups", "video", "fsdp"), None, None, None),
        P(None, None, "fsdp", None),
        P(),
        P(),
        P(None, "fsdp", None),
    )
    return jax.shard_map(
        body,
        mesh=mesh,
        in_specs=placed,
        out_specs=P(("groups", "video", "fsdp"), None, None, None),
        check_vma=False,
    )
```

```python
import functools

import jax
import jax.numpy as jnp
from jax import lax
from jax.experimental import pallas as pl
from jax.experimental.pallas import tpu as pltpu
from jax.sharding import PartitionSpec as P

GROUPS = 32
CLIP = 16
MESH = pl.DeviceIdType.MESH
CHUNK = 256
PARTS = 1


def kernel(
    width,
    group_size,
    video_ref,
    ws_ref,
    gain_hbm,
    shift_hbm,
    wt_ref,
    out_ref,
    raw,
    xs,
    ws,
    wt,
    acc,
    hid,
    near,
    gain_ref,
    shift_ref,
    far_raw,
    far_xs,
    stats,
    far_stats,
    far_hid,
    local_sem,
    w_send,
    w_recv,
    near_send,
    near_recv,
    far_send,
    far_recv,
    stat_send,
    stat_recv,
    late_send,
    late_recv,
):
    rows = raw.shape[0]
    half = wt.shape[2]
    blocks = 2
    group = lax.axis_index("groups")
    block = lax.axis_index("video")
    side = lax.axis_index("fsdp")
    other = 1 - side
    position = (block * 2 + side) % CLIP
    has_far = position != side * (CLIP - 1)
    partner = (group, block, other)
    far_block = jnp.where(has_far, block + 2 * side - 1, block)
    distant = (group, far_block, other)

    video_copy = pltpu.make_async_copy(video_ref, raw, local_sem.at[0])
    ws_copy = pltpu.make_async_copy(ws_ref, ws.at[side], local_sem.at[1])
    wt_copy = pltpu.make_async_copy(wt_ref, wt.at[side], local_sem.at[2])
    gain_copy = pltpu.make_async_copy(gain_hbm, gain_ref, local_sem.at[3])
    shift_copy = pltpu.make_async_copy(shift_hbm, shift_ref, local_sem.at[4])
    video_copy.start()
    ws_copy.start()
    wt_copy.start()
    gain_copy.start()
    shift_copy.start()

    barrier = pltpu.get_barrier_semaphore()
    pl.semaphore_signal(barrier, inc=1, device_id=partner, device_id_type=MESH)

    @pl.when(has_far)
    def _():
        pl.semaphore_signal(barrier, inc=1, device_id=distant, device_id_type=MESH)

    pl.semaphore_wait(barrier, 1 + has_far.astype(jnp.int32))

    early = rows // 2
    step_rows = early // PARTS
    bounds = [0] + [step_rows * (p + 1) + width for p in range(PARTS)]
    far_copies = []
    for p in range(PARTS):
        span = pl.ds(bounds[p], bounds[p + 1] - bounds[p])
        far_copies.append(
            pltpu.make_async_remote_copy(
                src_ref=video_ref.at[span],
                dst_ref=far_raw.at[span],
                send_sem=far_send.at[p],
                recv_sem=far_recv.at[p],
                device_id=distant,
                device_id_type=MESH,
            )
        )

    @pl.when(has_far)
    def _():
        for copy in far_copies:
            copy.start()

    w_copies = []
    for nb in range(blocks):
        columns = pl.ds(nb * half, half)
        w_copies.append(
            pltpu.make_async_remote_copy(
                src_ref=ws_ref.at[:, columns],
                dst_ref=ws.at[side, :, columns],
                send_sem=w_send.at[nb],
                recv_sem=w_recv.at[nb],
                device_id=partner,
                device_id_type=MESH,
            )
        )
    w_copies.append(
        pltpu.make_async_remote_copy(
            src_ref=wt_ref,
            dst_ref=wt.at[side],
            send_sem=w_send.at[blocks],
            recv_sem=w_recv.at[blocks],
            device_id=partner,
            device_id_type=MESH,
        )
    )
    for copy in w_copies:
        copy.start()

    video_copy.wait()

    def taps(source, target, low, high):
        count = high - low
        column = lax.broadcasted_iota(jnp.int32, (count, half), 0) % width
        for h in range(blocks):
            centre = source[low:high, h * half : (h + 1) * half]
            wide = centre.astype(jnp.float32)
            before = jnp.where(column != 0, pltpu.roll(wide, 1, 0), 0.0)
            after = jnp.where(column != width - 1, pltpu.roll(wide, count - 1, 0), 0.0)
            here = slice(width + low, width + high)
            target[h, here, 0:half] = before.astype(jnp.bfloat16)
            target[h, here, half : 2 * half] = centre
            target[h, here, 2 * half : 3 * half] = after.astype(jnp.bfloat16)

    def edges(target):
        edge = jnp.zeros((width, 3 * half), jnp.bfloat16)
        for h in range(blocks):
            target[h, 0:width, :] = edge
            target[h, width + rows : 2 * width + rows, :] = edge

    edges(xs)
    for h in range(blocks):
        far_xs[h, 0:width, :] = jnp.zeros((width, 3 * half), jnp.bfloat16)
    taps(raw, xs, 0, rows)

    def windows(source, h, start, count):
        return jnp.concatenate(
            [source[h, pl.ds(start + dy * width, count), :] for dy in range(3)], axis=1
        )

    def conv(h, nb, first):
        def step(m, carry):
            start = pl.multiple_of(m * CHUNK, CHUNK)
            total = jnp.dot(
                windows(xs, h, start, CHUNK),
                ws[h, :, nb * half : (nb + 1) * half],
                preferred_element_type=jnp.float32,
            )
            if not first:
                total = total + acc[nb, pl.ds(start, CHUNK), :]
            acc[nb, pl.ds(start, CHUNK), :] = total
            return carry

        lax.fori_loop(0, rows // CHUNK, step, 0)

    ws_copy.wait()
    for nb in range(blocks):
        conv(side, nb, True)

    same = (
        lax.broadcasted_iota(jnp.int32, (half, half), 0) // group_size
        == lax.broadcasted_iota(jnp.int32, (half, half), 1) // group_size
    ).astype(jnp.float32)

    def spread(sums):
        wide = jnp.broadcast_to(sums, (8, half))
        total = jnp.dot(
            wide, same, preferred_element_type=jnp.float32, precision=lax.Precision.HIGHEST
        )
        return total[0:1] / (rows * group_size)

    stat_copies, late_copies = [], []
    for nb in range(blocks):
        stat_copies.append(
            pltpu.make_async_remote_copy(
                src_ref=stats.at[nb],
                dst_ref=far_stats.at[nb],
                send_sem=stat_send.at[nb],
                recv_sem=stat_recv.at[nb],
                device_id=distant,
                device_id_type=MESH,
            )
        )
        late_copies.append(
            pltpu.make_async_remote_copy(
                src_ref=hid.at[nb, pl.ds(early, rows - early)],
                dst_ref=far_hid.at[nb],
                send_sem=late_send.at[nb],
                recv_sem=late_recv.at[nb],
                device_id=distant,
                device_id_type=MESH,
            )
        )
    gain_copy.wait()
    shift_copy.wait()
    h_copies = []
    for nb in range(blocks):
        w_copies[nb].wait_recv()
        conv(other, nb, False)
        mean = spread(jnp.sum(acc[nb], axis=0, keepdims=True))
        variance = spread(jnp.sum(jnp.square(acc[nb] - mean), axis=0, keepdims=True))
        span = slice(nb * half, (nb + 1) * half)
        scale = lax.rsqrt(variance + 1e-05) * gain_ref[:, span]
        stats[nb, 0] = jnp.broadcast_to(mean, (8, half))
        stats[nb, 1] = jnp.broadcast_to(scale, (8, half))

        @pl.when(has_far)
        def _():
            stat_copies[nb].start()

        v = (acc[nb] - mean) * scale + shift_ref[:, span]
        hid[nb] = (v / (1.0 + jnp.exp(-v))).astype(jnp.bfloat16)

        @pl.when(has_far)
        def _():
            late_copies[nb].start()

        near_copy = pltpu.make_async_remote_copy(
            src_ref=hid.at[nb],
            dst_ref=near.at[nb],
            send_sem=near_send.at[nb],
            recv_sem=near_recv.at[nb],
            device_id=partner,
            device_id_type=MESH,
        )
        near_copy.start()
        h_copies.append(near_copy)

    def mix(frame, tap, nb):
        def step(m, carry):
            spot = pl.ds(pl.multiple_of(m * CHUNK, CHUNK), CHUNK)
            for ob in range(blocks):
                part = jnp.dot(
                    frame[nb, spot, :],
                    wt[nb, tap, :, ob * half : (ob + 1) * half],
                    preferred_element_type=jnp.float32,
                )
                acc[ob, spot, :] = acc[ob, spot, :] + part
            return carry

        lax.fori_loop(0, rows // CHUNK, step, 0)

    wt_copy.wait()
    w_copies[blocks].wait_recv()
    for nb in range(blocks):
        acc[nb] = hid[nb].astype(jnp.float32)
    for nb in range(blocks):
        mix(hid, 1, nb)

    def far_part(p):
        far_copies[p].wait_recv()
        taps(far_raw, far_xs, bounds[p], bounds[p + 1])
        low = p * step_rows
        here = slice(low, low + step_rows)
        for nb in range(blocks):
            if p == 0:
                stat_copies[nb].wait_recv()
            total = jnp.dot(
                windows(far_xs, 0, low, step_rows),
                ws[0, :, nb * half : (nb + 1) * half],
                preferred_element_type=jnp.float32,
            ) + jnp.dot(
                windows(far_xs, 1, low, step_rows),
                ws[1, :, nb * half : (nb + 1) * half],
                preferred_element_type=jnp.float32,
            )
            v = (total - far_stats[nb, 0, 0:1]) * far_stats[nb, 1, 0:1]
            v = v + shift_ref[:, nb * half : (nb + 1) * half]
            frame = (v / (1.0 + jnp.exp(-v))).astype(jnp.bfloat16)
            for ob in range(blocks):
                acc[ob, here, :] = acc[ob, here, :] + jnp.dot(
                    frame,
                    wt[nb, 2 * side, :, ob * half : (ob + 1) * half],
                    preferred_element_type=jnp.float32,
                )

    for nb in range(blocks):
        h_copies[nb].wait_recv()
        mix(near, 2 * other, nb)

    @pl.when(has_far)
    def _():
        for p in range(PARTS):
            far_part(p)
        for nb in range(blocks):
            late_copies[nb].wait_recv()
            for ob in range(blocks):
                acc[ob, early:rows, :] = acc[ob, early:rows, :] + jnp.dot(
                    far_hid[nb],
                    wt[nb, 2 * side, :, ob * half : (ob + 1) * half],
                    preferred_element_type=jnp.float32,
                )

    for nb in range(blocks):
        out_ref[:, nb * half : (nb + 1) * half] = acc[nb].astype(jnp.bfloat16)

    for copy in w_copies + h_copies:
        copy.wait_send()

    @pl.when(has_far)
    def _():
        for copy in far_copies + stat_copies + late_copies:
            copy.wait_send()


def body(video, w_spatial, norm_gain, norm_shift, w_time):
    count, height, width, channels = video.shape
    half = w_time.shape[1]
    assert count == 1 and 2 * half == channels
    rows = height * width
    bf16 = jnp.bfloat16
    vmem = pl.BlockSpec(memory_space=pltpu.VMEM)
    hbm = pl.BlockSpec(memory_space=pltpu.HBM)
    dma = pltpu.SemaphoreType.DMA
    out = pl.pallas_call(
        functools.partial(kernel, width, channels // GROUPS),
        out_shape=jax.ShapeDtypeStruct((rows, channels), bf16),
        in_specs=[hbm] * 5,
        out_specs=vmem,
        scratch_shapes=[
            pltpu.VMEM((rows, channels), bf16),
            pltpu.VMEM((2, rows + 2 * width, 3 * half), bf16),
            pltpu.VMEM((2, 9 * half, channels), bf16),
            pltpu.VMEM((2, 3, half, channels), bf16),
            pltpu.VMEM((2, rows, half), jnp.float32),
            pltpu.VMEM((2, rows, half), bf16),
            pltpu.VMEM((2, rows, half), bf16),
            pltpu.VMEM((1, channels), jnp.float32),
            pltpu.VMEM((1, channels), jnp.float32),
            pltpu.VMEM((rows // 2 + width, channels), bf16),
            pltpu.VMEM((2, rows // 2 + 2 * width, 3 * half), bf16),
            pltpu.VMEM((2, 2, 8, half), jnp.float32),
            pltpu.VMEM((2, 2, 8, half), jnp.float32),
            pltpu.VMEM((2, rows - rows // 2, half), bf16),
            dma((5,)),
            dma((3,)),
            dma((3,)),
            dma((2,)),
            dma((2,)),
            dma((PARTS,)),
            dma((PARTS,)),
            dma((2,)),
            dma((2,)),
            dma((2,)),
            dma((2,)),
        ],
        compiler_params=pltpu.CompilerParams(
            collective_id=0, has_side_effects=True, vmem_limit_bytes=48 * 1024 * 1024
        ),
    )(
        *[
            pltpu.with_memory_space_constraint(array, pltpu.HBM)
            for array in (
                video.reshape(rows, channels),
                w_spatial.reshape(9 * half, channels),
                norm_gain.reshape(1, channels),
                norm_shift.reshape(1, channels),
                w_time,
            )
        ]
    )
    return out.reshape(video.shape)


def solution(mesh):
    placed = (
        P(("groups", "video", "fsdp"), None, None, None),
        P(None, None, "fsdp", None),
        P(),
        P(),
        P(None, "fsdp", None),
    )
    return jax.shard_map(
        body,
        mesh=mesh,
        in_specs=placed,
        out_specs=P(("groups", "video", "fsdp"), None, None, None),
        check_vma=False,
    )
```

```python
import functools

import jax
import jax.numpy as jnp
from jax import lax
from jax.experimental import pallas as pl
from jax.experimental.pallas import tpu as pltpu
from jax.sharding import PartitionSpec as P

GROUPS = 32
CLIP = 16
MESH = pl.DeviceIdType.MESH
CHUNK = 256
PARTS = 1


def kernel(
    width,
    group_size,
    video_ref,
    ws_ref,
    gain_hbm,
    shift_hbm,
    wt_ref,
    out_ref,
    raw,
    xs,
    ws,
    wt,
    acc,
    hid,
    near,
    gain_ref,
    shift_ref,
    far_raw,
    far_xs,
    stats,
    far_stats,
    far_hid,
    local_sem,
    w_send,
    w_recv,
    near_send,
    near_recv,
    far_send,
    far_recv,
    stat_send,
    stat_recv,
    late_send,
    late_recv,
):
    rows = raw.shape[0]
    half = wt.shape[2]
    blocks = 2
    group = lax.axis_index("groups")
    block = lax.axis_index("video")
    side = lax.axis_index("fsdp")
    other = 1 - side
    position = (block * 2 + side) % CLIP
    has_far = position != side * (CLIP - 1)
    partner = (group, block, other)
    far_block = jnp.where(has_far, block + 2 * side - 1, block)
    distant = (group, far_block, other)

    video_copy = pltpu.make_async_copy(video_ref, raw, local_sem.at[0])
    ws_copy = pltpu.make_async_copy(ws_ref, ws.at[side], local_sem.at[1])
    wt_copy = pltpu.make_async_copy(wt_ref, wt.at[side], local_sem.at[2])
    gain_copy = pltpu.make_async_copy(gain_hbm, gain_ref, local_sem.at[3])
    shift_copy = pltpu.make_async_copy(shift_hbm, shift_ref, local_sem.at[4])
    video_copy.start()
    ws_copy.start()
    wt_copy.start()
    gain_copy.start()
    shift_copy.start()

    barrier = pltpu.get_barrier_semaphore()
    pl.semaphore_signal(barrier, inc=1, device_id=partner, device_id_type=MESH)

    @pl.when(has_far)
    def _():
        pl.semaphore_signal(barrier, inc=1, device_id=distant, device_id_type=MESH)

    pl.semaphore_wait(barrier, 1 + has_far.astype(jnp.int32))

    early = rows // 2
    step_rows = early // PARTS
    bounds = [0] + [step_rows * (p + 1) + width for p in range(PARTS)]
    far_copies = []
    for p in range(PARTS):
        span = pl.ds(bounds[p], bounds[p + 1] - bounds[p])
        far_copies.append(
            pltpu.make_async_remote_copy(
                src_ref=video_ref.at[span],
                dst_ref=far_raw.at[span],
                send_sem=far_send.at[p],
                recv_sem=far_recv.at[p],
                device_id=distant,
                device_id_type=MESH,
            )
        )

    @pl.when(has_far)
    def _():
        for copy in far_copies:
            copy.start()

    w_copies = []
    for nb in range(blocks):
        columns = pl.ds(nb * half, half)
        w_copies.append(
            pltpu.make_async_remote_copy(
                src_ref=ws_ref.at[:, columns],
                dst_ref=ws.at[side, :, columns],
                send_sem=w_send.at[nb],
                recv_sem=w_recv.at[nb],
                device_id=partner,
                device_id_type=MESH,
            )
        )
    w_copies.append(
        pltpu.make_async_remote_copy(
            src_ref=wt_ref,
            dst_ref=wt.at[side],
            send_sem=w_send.at[blocks],
            recv_sem=w_recv.at[blocks],
            device_id=partner,
            device_id_type=MESH,
        )
    )
    for copy in w_copies:
        copy.start()

    video_copy.wait()

    def taps(source, target, low, high):
        count = high - low
        column = lax.broadcasted_iota(jnp.int32, (count, half), 0) % width
        for h in range(blocks):
            centre = source[low:high, h * half : (h + 1) * half]
            wide = centre.astype(jnp.float32)
            before = jnp.where(column != 0, pltpu.roll(wide, 1, 0), 0.0)
            after = jnp.where(column != width - 1, pltpu.roll(wide, count - 1, 0), 0.0)
            here = slice(width + low, width + high)
            target[h, here, 0:half] = before.astype(jnp.bfloat16)
            target[h, here, half : 2 * half] = centre
            target[h, here, 2 * half : 3 * half] = after.astype(jnp.bfloat16)

    def edges(target):
        edge = jnp.zeros((width, 3 * half), jnp.bfloat16)
        for h in range(blocks):
            target[h, 0:width, :] = edge
            target[h, width + rows : 2 * width + rows, :] = edge

    edges(xs)
    for h in range(blocks):
        far_xs[h, 0:width, :] = jnp.zeros((width, 3 * half), jnp.bfloat16)
    taps(raw, xs, 0, rows)

    def windows(source, h, start, count):
        return jnp.concatenate(
            [source[h, pl.ds(start + dy * width, count), :] for dy in range(3)], axis=1
        )

    def conv(h, nb, first):
        def step(m, carry):
            start = pl.multiple_of(m * CHUNK, CHUNK)
            total = jnp.dot(
                windows(xs, h, start, CHUNK),
                ws[h, :, nb * half : (nb + 1) * half],
                preferred_element_type=jnp.float32,
            )
            if not first:
                total = total + acc[nb, pl.ds(start, CHUNK), :]
            acc[nb, pl.ds(start, CHUNK), :] = total
            return carry

        lax.fori_loop(0, rows // CHUNK, step, 0)

    ws_copy.wait()
    for nb in range(blocks):
        conv(side, nb, True)

    same = (
        lax.broadcasted_iota(jnp.int32, (half, half), 0) // group_size
        == lax.broadcasted_iota(jnp.int32, (half, half), 1) // group_size
    ).astype(jnp.float32)

    def spread(sums):
        wide = jnp.broadcast_to(sums, (8, half))
        total = jnp.dot(
            wide, same, preferred_element_type=jnp.float32, precision=lax.Precision.HIGHEST
        )
        return total[0:1] / (rows * group_size)

    stat_copies, late_copies = [], []
    for nb in range(blocks):
        stat_copies.append(
            pltpu.make_async_remote_copy(
                src_ref=stats.at[nb],
                dst_ref=far_stats.at[nb],
                send_sem=stat_send.at[nb],
                recv_sem=stat_recv.at[nb],
                device_id=distant,
                device_id_type=MESH,
            )
        )
        late_copies.append(
            pltpu.make_async_remote_copy(
                src_ref=hid.at[nb, pl.ds(early, rows - early)],
                dst_ref=far_hid.at[nb],
                send_sem=late_send.at[nb],
                recv_sem=late_recv.at[nb],
                device_id=distant,
                device_id_type=MESH,
            )
        )
    gain_copy.wait()
    shift_copy.wait()
    h_copies = []
    for nb in range(blocks):
        w_copies[nb].wait_recv()
        conv(other, nb, False)
        mean = spread(jnp.sum(acc[nb], axis=0, keepdims=True))
        variance = spread(jnp.sum(jnp.square(acc[nb] - mean), axis=0, keepdims=True))
        span = slice(nb * half, (nb + 1) * half)
        scale = lax.rsqrt(variance + 1e-05) * gain_ref[:, span]
        stats[nb, 0] = jnp.broadcast_to(mean, (8, half))
        stats[nb, 1] = jnp.broadcast_to(scale, (8, half))

        @pl.when(has_far)
        def _():
            stat_copies[nb].start()

        v = (acc[nb] - mean) * scale + shift_ref[:, span]
        hid[nb] = (v / (1.0 + jnp.exp(-v))).astype(jnp.bfloat16)

        @pl.when(has_far)
        def _():
            late_copies[nb].start()

        near_copy = pltpu.make_async_remote_copy(
            src_ref=hid.at[nb],
            dst_ref=near.at[nb],
            send_sem=near_send.at[nb],
            recv_sem=near_recv.at[nb],
            device_id=partner,
            device_id_type=MESH,
        )
        near_copy.start()
        h_copies.append(near_copy)

    def mix(frame, tap, nb):
        def step(m, carry):
            spot = pl.ds(pl.multiple_of(m * CHUNK, CHUNK), CHUNK)
            for ob in range(blocks):
                part = jnp.dot(
                    frame[nb, spot, :],
                    wt[nb, tap, :, ob * half : (ob + 1) * half],
                    preferred_element_type=jnp.float32,
                )
                acc[ob, spot, :] = acc[ob, spot, :] + part
            return carry

        lax.fori_loop(0, rows // CHUNK, step, 0)

    wt_copy.wait()
    w_copies[blocks].wait_recv()
    for nb in range(blocks):
        acc[nb] = hid[nb].astype(jnp.float32)
    for nb in range(blocks):
        mix(hid, 1, nb)

    def far_part(p):
        far_copies[p].wait_recv()
        taps(far_raw, far_xs, bounds[p], bounds[p + 1])
        low = p * step_rows
        here = slice(low, low + step_rows)
        for nb in range(blocks):
            if p == 0:
                stat_copies[nb].wait_recv()
            total = jnp.dot(
                windows(far_xs, 0, low, step_rows),
                ws[0, :, nb * half : (nb + 1) * half],
                preferred_element_type=jnp.float32,
            ) + jnp.dot(
                windows(far_xs, 1, low, step_rows),
                ws[1, :, nb * half : (nb + 1) * half],
                preferred_element_type=jnp.float32,
            )
            v = (total - far_stats[nb, 0, 0:1]) * far_stats[nb, 1, 0:1]
            v = v + shift_ref[:, nb * half : (nb + 1) * half]
            frame = (v / (1.0 + jnp.exp(-v))).astype(jnp.bfloat16)
            for ob in range(blocks):
                acc[ob, here, :] = acc[ob, here, :] + jnp.dot(
                    frame,
                    wt[nb, 2 * side, :, ob * half : (ob + 1) * half],
                    preferred_element_type=jnp.float32,
                )

    for nb in range(blocks):
        h_copies[nb].wait_recv()
        mix(near, 2 * other, nb)

    @pl.when(has_far)
    def _():
        for p in range(PARTS):
            far_part(p)

    def emit(low, high):
        for nb in range(blocks):
            part = acc[nb, low:high, :].astype(jnp.bfloat16)
            out_ref[low:high, nb * half : (nb + 1) * half] = part

    emit(0, early)

    @pl.when(has_far)
    def _():
        for nb in range(blocks):
            late_copies[nb].wait_recv()
            for ob in range(blocks):
                acc[ob, early:rows, :] = acc[ob, early:rows, :] + jnp.dot(
                    far_hid[nb],
                    wt[nb, 2 * side, :, ob * half : (ob + 1) * half],
                    preferred_element_type=jnp.float32,
                )

    emit(early, rows)

    for copy in w_copies + h_copies:
        copy.wait_send()

    @pl.when(has_far)
    def _():
        for copy in far_copies + stat_copies + late_copies:
            copy.wait_send()


def body(video, w_spatial, norm_gain, norm_shift, w_time):
    count, height, width, channels = video.shape
    half = w_time.shape[1]
    assert count == 1 and 2 * half == channels
    rows = height * width
    bf16 = jnp.bfloat16
    vmem = pl.BlockSpec(memory_space=pltpu.VMEM)
    hbm = pl.BlockSpec(memory_space=pltpu.HBM)
    dma = pltpu.SemaphoreType.DMA
    out = pl.pallas_call(
        functools.partial(kernel, width, channels // GROUPS),
        out_shape=jax.ShapeDtypeStruct((rows, channels), bf16),
        in_specs=[hbm] * 5,
        out_specs=vmem,
        scratch_shapes=[
            pltpu.VMEM((rows, channels), bf16),
            pltpu.VMEM((2, rows + 2 * width, 3 * half), bf16),
            pltpu.VMEM((2, 9 * half, channels), bf16),
            pltpu.VMEM((2, 3, half, channels), bf16),
            pltpu.VMEM((2, rows, half), jnp.float32),
            pltpu.VMEM((2, rows, half), bf16),
            pltpu.VMEM((2, rows, half), bf16),
            pltpu.VMEM((1, channels), jnp.float32),
            pltpu.VMEM((1, channels), jnp.float32),
            pltpu.VMEM((rows // 2 + width, channels), bf16),
            pltpu.VMEM((2, rows // 2 + 2 * width, 3 * half), bf16),
            pltpu.VMEM((2, 2, 8, half), jnp.float32),
            pltpu.VMEM((2, 2, 8, half), jnp.float32),
            pltpu.VMEM((2, rows - rows // 2, half), bf16),
            dma((5,)),
            dma((3,)),
            dma((3,)),
            dma((2,)),
            dma((2,)),
            dma((PARTS,)),
            dma((PARTS,)),
            dma((2,)),
            dma((2,)),
            dma((2,)),
            dma((2,)),
        ],
        compiler_params=pltpu.CompilerParams(
            collective_id=0, has_side_effects=True, vmem_limit_bytes=48 * 1024 * 1024
        ),
    )(
        *[
            pltpu.with_memory_space_constraint(array, pltpu.HBM)
            for array in (
                video.reshape(rows, channels),
                w_spatial.reshape(9 * half, channels),
                norm_gain.reshape(1, channels),
                norm_shift.reshape(1, channels),
                w_time,
            )
        ]
    )
    return out.reshape(video.shape)


def solution(mesh):
    placed = (
        P(("groups", "video", "fsdp"), None, None, None),
        P(None, None, "fsdp", None),
        P(),
        P(),
        P(None, "fsdp", None),
    )
    return jax.shard_map(
        body,
        mesh=mesh,
        in_specs=placed,
        out_specs=P(("groups", "video", "fsdp"), None, None, None),
        check_vma=False,
    )
```

```python
import functools

import jax
import jax.numpy as jnp
from jax import lax
from jax.experimental import pallas as pl
from jax.experimental.pallas import tpu as pltpu
from jax.sharding import PartitionSpec as P

GROUPS = 32
CLIP = 16
MESH = pl.DeviceIdType.MESH
CHUNK = 256
PARTS = 1


def kernel(
    width,
    group_size,
    video_ref,
    ws_ref,
    gain_hbm,
    shift_hbm,
    wt_ref,
    out_ref,
    raw,
    xs,
    ws,
    wt,
    acc,
    hid,
    near,
    gain_ref,
    shift_ref,
    far_raw,
    far_xs,
    stats,
    far_stats,
    far_hid,
    local_sem,
    w_send,
    w_recv,
    near_send,
    near_recv,
    far_send,
    far_recv,
    stat_send,
    stat_recv,
    late_send,
    late_recv,
):
    rows = raw.shape[0]
    half = wt.shape[2]
    blocks = 2
    group = lax.axis_index("groups")
    block = lax.axis_index("video")
    side = lax.axis_index("fsdp")
    other = 1 - side
    position = (block * 2 + side) % CLIP
    has_far = position != side * (CLIP - 1)
    partner = (group, block, other)
    far_block = jnp.where(has_far, block + 2 * side - 1, block)
    distant = (group, far_block, other)

    video_copy = pltpu.make_async_copy(video_ref, raw, local_sem.at[0])
    ws_copy = pltpu.make_async_copy(ws_ref, ws.at[side], local_sem.at[1])
    wt_copy = pltpu.make_async_copy(wt_ref, wt.at[side], local_sem.at[2])
    gain_copy = pltpu.make_async_copy(gain_hbm, gain_ref, local_sem.at[3])
    shift_copy = pltpu.make_async_copy(shift_hbm, shift_ref, local_sem.at[4])
    video_copy.start()
    ws_copy.start()
    wt_copy.start()
    gain_copy.start()
    shift_copy.start()

    barrier = pltpu.get_barrier_semaphore()
    pl.semaphore_signal(barrier, inc=1, device_id=partner, device_id_type=MESH)

    @pl.when(has_far)
    def _():
        pl.semaphore_signal(barrier, inc=1, device_id=distant, device_id_type=MESH)

    pl.semaphore_wait(barrier, 1 + has_far.astype(jnp.int32))

    early = rows * 5 // 8
    step_rows = early // PARTS
    bounds = [0] + [step_rows * (p + 1) + width for p in range(PARTS)]
    far_copies = []
    for p in range(PARTS):
        span = pl.ds(bounds[p], bounds[p + 1] - bounds[p])
        far_copies.append(
            pltpu.make_async_remote_copy(
                src_ref=video_ref.at[span],
                dst_ref=far_raw.at[span],
                send_sem=far_send.at[p],
                recv_sem=far_recv.at[p],
                device_id=distant,
                device_id_type=MESH,
            )
        )

    @pl.when(has_far)
    def _():
        for copy in far_copies:
            copy.start()

    w_copies = []
    for nb in range(blocks):
        columns = pl.ds(nb * half, half)
        w_copies.append(
            pltpu.make_async_remote_copy(
                src_ref=ws_ref.at[:, columns],
                dst_ref=ws.at[side, :, columns],
                send_sem=w_send.at[nb],
                recv_sem=w_recv.at[nb],
                device_id=partner,
                device_id_type=MESH,
            )
        )
    w_copies.append(
        pltpu.make_async_remote_copy(
            src_ref=wt_ref,
            dst_ref=wt.at[side],
            send_sem=w_send.at[blocks],
            recv_sem=w_recv.at[blocks],
            device_id=partner,
            device_id_type=MESH,
        )
    )
    for copy in w_copies:
        copy.start()

    video_copy.wait()

    def taps(source, target, low, high):
        count = high - low
        column = lax.broadcasted_iota(jnp.int32, (count, half), 0) % width
        for h in range(blocks):
            centre = source[low:high, h * half : (h + 1) * half]
            wide = centre.astype(jnp.float32)
            before = jnp.where(column != 0, pltpu.roll(wide, 1, 0), 0.0)
            after = jnp.where(column != width - 1, pltpu.roll(wide, count - 1, 0), 0.0)
            here = slice(width + low, width + high)
            target[h, here, 0:half] = before.astype(jnp.bfloat16)
            target[h, here, half : 2 * half] = centre
            target[h, here, 2 * half : 3 * half] = after.astype(jnp.bfloat16)

    def edges(target):
        edge = jnp.zeros((width, 3 * half), jnp.bfloat16)
        for h in range(blocks):
            target[h, 0:width, :] = edge
            target[h, width + rows : 2 * width + rows, :] = edge

    edges(xs)
    for h in range(blocks):
        far_xs[h, 0:width, :] = jnp.zeros((width, 3 * half), jnp.bfloat16)
    taps(raw, xs, 0, rows)

    def windows(source, h, start, count):
        return jnp.concatenate(
            [source[h, pl.ds(start + dy * width, count), :] for dy in range(3)], axis=1
        )

    def conv(h, nb, first):
        def step(m, carry):
            start = pl.multiple_of(m * CHUNK, CHUNK)
            total = jnp.dot(
                windows(xs, h, start, CHUNK),
                ws[h, :, nb * half : (nb + 1) * half],
                preferred_element_type=jnp.float32,
            )
            if not first:
                total = total + acc[nb, pl.ds(start, CHUNK), :]
            acc[nb, pl.ds(start, CHUNK), :] = total
            return carry

        lax.fori_loop(0, rows // CHUNK, step, 0)

    ws_copy.wait()
    for nb in range(blocks):
        conv(side, nb, True)

    same = (
        lax.broadcasted_iota(jnp.int32, (half, half), 0) // group_size
        == lax.broadcasted_iota(jnp.int32, (half, half), 1) // group_size
    ).astype(jnp.float32)

    def spread(sums):
        wide = jnp.broadcast_to(sums, (8, half))
        total = jnp.dot(
            wide, same, preferred_element_type=jnp.float32, precision=lax.Precision.HIGHEST
        )
        return total[0:1] / (rows * group_size)

    stat_copies, late_copies = [], []
    for nb in range(blocks):
        stat_copies.append(
            pltpu.make_async_remote_copy(
                src_ref=stats.at[nb],
                dst_ref=far_stats.at[nb],
                send_sem=stat_send.at[nb],
                recv_sem=stat_recv.at[nb],
                device_id=distant,
                device_id_type=MESH,
            )
        )
        late_copies.append(
            pltpu.make_async_remote_copy(
                src_ref=hid.at[nb, pl.ds(early, rows - early)],
                dst_ref=far_hid.at[nb],
                send_sem=late_send.at[nb],
                recv_sem=late_recv.at[nb],
                device_id=distant,
                device_id_type=MESH,
            )
        )
    gain_copy.wait()
    shift_copy.wait()
    h_copies = []
    for nb in range(blocks):
        w_copies[nb].wait_recv()
        conv(other, nb, False)
        mean = spread(jnp.sum(acc[nb], axis=0, keepdims=True))
        variance = spread(jnp.sum(jnp.square(acc[nb] - mean), axis=0, keepdims=True))
        span = slice(nb * half, (nb + 1) * half)
        scale = lax.rsqrt(variance + 1e-05) * gain_ref[:, span]
        stats[nb, 0] = jnp.broadcast_to(mean, (8, half))
        stats[nb, 1] = jnp.broadcast_to(scale, (8, half))

        @pl.when(has_far)
        def _():
            stat_copies[nb].start()

        v = (acc[nb] - mean) * scale + shift_ref[:, span]
        hid[nb] = (v / (1.0 + jnp.exp(-v))).astype(jnp.bfloat16)

        @pl.when(has_far)
        def _():
            late_copies[nb].start()

        near_copy = pltpu.make_async_remote_copy(
            src_ref=hid.at[nb],
            dst_ref=near.at[nb],
            send_sem=near_send.at[nb],
            recv_sem=near_recv.at[nb],
            device_id=partner,
            device_id_type=MESH,
        )
        near_copy.start()
        h_copies.append(near_copy)

    def mix(frame, tap, nb):
        def step(m, carry):
            spot = pl.ds(pl.multiple_of(m * CHUNK, CHUNK), CHUNK)
            for ob in range(blocks):
                part = jnp.dot(
                    frame[nb, spot, :],
                    wt[nb, tap, :, ob * half : (ob + 1) * half],
                    preferred_element_type=jnp.float32,
                )
                acc[ob, spot, :] = acc[ob, spot, :] + part
            return carry

        lax.fori_loop(0, rows // CHUNK, step, 0)

    wt_copy.wait()
    w_copies[blocks].wait_recv()
    for nb in range(blocks):
        acc[nb] = hid[nb].astype(jnp.float32)
    for nb in range(blocks):
        mix(hid, 1, nb)

    def far_part(p):
        far_copies[p].wait_recv()
        taps(far_raw, far_xs, bounds[p], bounds[p + 1])
        low = p * step_rows
        here = slice(low, low + step_rows)
        for nb in range(blocks):
            if p == 0:
                stat_copies[nb].wait_recv()
            total = jnp.dot(
                windows(far_xs, 0, low, step_rows),
                ws[0, :, nb * half : (nb + 1) * half],
                preferred_element_type=jnp.float32,
            ) + jnp.dot(
                windows(far_xs, 1, low, step_rows),
                ws[1, :, nb * half : (nb + 1) * half],
                preferred_element_type=jnp.float32,
            )
            v = (total - far_stats[nb, 0, 0:1]) * far_stats[nb, 1, 0:1]
            v = v + shift_ref[:, nb * half : (nb + 1) * half]
            frame = (v / (1.0 + jnp.exp(-v))).astype(jnp.bfloat16)
            for ob in range(blocks):
                acc[ob, here, :] = acc[ob, here, :] + jnp.dot(
                    frame,
                    wt[nb, 2 * side, :, ob * half : (ob + 1) * half],
                    preferred_element_type=jnp.float32,
                )

    for nb in range(blocks):
        h_copies[nb].wait_recv()
        mix(near, 2 * other, nb)

    @pl.when(has_far)
    def _():
        for p in range(PARTS):
            far_part(p)

    def emit(low, high):
        for nb in range(blocks):
            part = acc[nb, low:high, :].astype(jnp.bfloat16)
            out_ref[low:high, nb * half : (nb + 1) * half] = part

    emit(0, early)

    @pl.when(has_far)
    def _():
        for nb in range(blocks):
            late_copies[nb].wait_recv()
            for ob in range(blocks):
                acc[ob, early:rows, :] = acc[ob, early:rows, :] + jnp.dot(
                    far_hid[nb],
                    wt[nb, 2 * side, :, ob * half : (ob + 1) * half],
                    preferred_element_type=jnp.float32,
                )

    emit(early, rows)

    for copy in w_copies + h_copies:
        copy.wait_send()

    @pl.when(has_far)
    def _():
        for copy in far_copies + stat_copies + late_copies:
            copy.wait_send()


def body(video, w_spatial, norm_gain, norm_shift, w_time):
    count, height, width, channels = video.shape
    half = w_time.shape[1]
    assert count == 1 and 2 * half == channels
    rows = height * width
    bf16 = jnp.bfloat16
    vmem = pl.BlockSpec(memory_space=pltpu.VMEM)
    hbm = pl.BlockSpec(memory_space=pltpu.HBM)
    dma = pltpu.SemaphoreType.DMA
    out = pl.pallas_call(
        functools.partial(kernel, width, channels // GROUPS),
        out_shape=jax.ShapeDtypeStruct((rows, channels), bf16),
        in_specs=[hbm] * 5,
        out_specs=vmem,
        scratch_shapes=[
            pltpu.VMEM((rows, channels), bf16),
            pltpu.VMEM((2, rows + 2 * width, 3 * half), bf16),
            pltpu.VMEM((2, 9 * half, channels), bf16),
            pltpu.VMEM((2, 3, half, channels), bf16),
            pltpu.VMEM((2, rows, half), jnp.float32),
            pltpu.VMEM((2, rows, half), bf16),
            pltpu.VMEM((2, rows, half), bf16),
            pltpu.VMEM((1, channels), jnp.float32),
            pltpu.VMEM((1, channels), jnp.float32),
            pltpu.VMEM((rows * 5 // 8 + width, channels), bf16),
            pltpu.VMEM((2, rows * 5 // 8 + 2 * width, 3 * half), bf16),
            pltpu.VMEM((2, 2, 8, half), jnp.float32),
            pltpu.VMEM((2, 2, 8, half), jnp.float32),
            pltpu.VMEM((2, rows - rows * 5 // 8, half), bf16),
            dma((5,)),
            dma((3,)),
            dma((3,)),
            dma((2,)),
            dma((2,)),
            dma((PARTS,)),
            dma((PARTS,)),
            dma((2,)),
            dma((2,)),
            dma((2,)),
            dma((2,)),
        ],
        compiler_params=pltpu.CompilerParams(
            collective_id=0, has_side_effects=True, vmem_limit_bytes=48 * 1024 * 1024
        ),
    )(
        *[
            pltpu.with_memory_space_constraint(array, pltpu.HBM)
            for array in (
                video.reshape(rows, channels),
                w_spatial.reshape(9 * half, channels),
                norm_gain.reshape(1, channels),
                norm_shift.reshape(1, channels),
                w_time,
            )
        ]
    )
    return out.reshape(video.shape)


def solution(mesh):
    placed = (
        P(("groups", "video", "fsdp"), None, None, None),
        P(None, None, "fsdp", None),
        P(),
        P(),
        P(None, "fsdp", None),
    )
    return jax.shard_map(
        body,
        mesh=mesh,
        in_specs=placed,
        out_specs=P(("groups", "video", "fsdp"), None, None, None),
        check_vma=False,
    )
```
